32 devices in a mesh: sph: 8 (over y, x, core), grp: 4 (over z).
Axes of the slice: x: 2, y: 2, z: 4, core: 2. Of those that a mesh axis runs over, the one named last changes fastest.
Arguments:
- pixel_features: bfloat16 [32768, 512], P(('sph', 'grp')), may hold values from -6 to 6
- tier_one_codes: bfloat16 [2048, 512], P(('sph', 'grp')), may hold values from -6 to 6
- tier_two_codes: bfloat16 [128, 512], P(('sph', 'grp')), may hold values from -6 to 6
- tier_three_codes: bfloat16 [8, 512], P('sph'), may hold values from -6 to 6
- tier_one_picks: int32 [2048, 16], P(('sph', 'grp')), may hold values from 0 to 2047, as said below
- tier_two_picks: int32 [2048, 16], P(('sph', 'grp')), may hold values from 0 to 127, as said below
- tier_three_picks: int32 [2048, 16], P(('sph', 'grp')), may hold values from 0 to 7, as said below
- probe_matrix: bfloat16 [3, 512, 512], replicated, may hold values from -0.25 to 0.25
- address_matrix: bfloat16 [3, 512, 512], replicated, may hold values from -0.25 to 0.25
- content_matrix: bfloat16 [3, 512, 512], replicated, may hold values from -0.25 to 0.25
- merge_matrix: bfloat16 [3, 512, 512], replicated, may hold values from -0.25 to 0.25
- expand_matrix: bfloat16 [3, 512, 1024], replicated, may hold values from -0.25 to 0.25
- shrink_matrix: bfloat16 [3, 1024, 512], replicated, may hold values from -0.1875 to 0.1875
- rescale_factors: float32 [3, 3, 512], replicated, may hold values from 0.25 to 1.75
- logit_scaling: float32 [3, 8], replicated, may hold values from 0.5 to 2
Outputs:
- encoded: bfloat16 [32768, 512], P(('sph', 'grp'))
The draws below stay inside these ranges and needn't reach their ends.
Inputs may be any that keep to these rules, and one draw needn't show every extreme that they name: `tier_one_picks`: entry 0 of block b's list is b, its own level-one parent; every entry lies within 64 of b. `tier_two_picks`: entry 0 of block b's list is b // 16, its level-two parent; every entry lies in the same aligned run of 16 level-two latents as entry 0. `tier_three_picks`: entry 0 of block b's list is b // 256, its level-three parent.
All inputs are finite; a program needn't handle non-finite values.
Results may differ from the reference program's by a relative error of at most 0.01.
Values may be sent and summed in bfloat16 or wider, within the bound.
A program may use at most 128 MiB of HBM per device.

```python
import math
import jax
import jax.numpy as jnp
from jax import lax

D = 512
HEADS_ALL = 8
FFL = 1024
LIST = 16
BLK_DEV = 64
NFINE = 32768
LAT1 = 2048
LAT2 = 128
LAT3 = 8
GROUP2 = 16


def draw_tier_one_picks(key, part):
    anchor = jnp.arange(LAT1, dtype=jnp.int32)[:, None]
    offsets = jax.random.randint(key, (LAT1, LIST), -BLK_DEV, BLK_DEV + 1, dtype=jnp.int32)
    offsets = jnp.concatenate([jnp.zeros((LAT1, 1), jnp.int32), offsets[:, 1:]], axis=1)
    return jnp.clip(anchor + offsets, 0, LAT1 - 1).astype(jnp.int32)


def draw_tier_two_picks(key, part):
    parent = (jnp.arange(LAT1, dtype=jnp.int32) // 16)[:, None]
    start_row = parent // GROUP2 * GROUP2
    picks = jax.random.randint(key, (LAT1, LIST), 0, GROUP2, dtype=jnp.int32) + start_row
    return jnp.concatenate([parent, picks[:, 1:]], axis=1).astype(jnp.int32)


def draw_tier_three_picks(key, part):
    parent = (jnp.arange(LAT1, dtype=jnp.int32) // 256)[:, None]
    picks = jax.random.randint(key, (LAT1, LIST), 0, LAT3, dtype=jnp.int32)
    return jnp.concatenate([parent, picks[:, 1:]], axis=1).astype(jnp.int32)


def levels(own_key, dims, shards, smallest, largest):
    gain = 1.0
    for axis_at, blocks in shards:
        steps = jax.random.uniform(jax.random.fold_in(jax.random.fold_in(own_key, 6), axis_at), (blocks,), jnp.float32, smallest / len(shards), largest / len(shards))
        gain = gain * jnp.repeat(jnp.exp(steps), dims[axis_at] // blocks).reshape((-1,) + (1,) * (len(dims) - 1 - axis_at))
    return gain


def normal_values(own_key, dims, scale, limit, cuts=(), held_as=jnp.bfloat16):
    values = scale * jax.random.normal(own_key, dims, jnp.float32)
    if cuts:
        values = values * levels(own_key, dims, cuts, -0.22, 0.18)
    return jnp.clip(values, -limit, limit).astype(held_as)


def setup_inputs(seed: int = 0) -> dict:
    streams_of = jax.random.split(jax.random.key(seed), 16)
    return {
        "pixel_features": normal_values(streams_of[0], (NFINE, D), 1.0, 6.0, ((0, 32),)),
        "tier_one_codes": normal_values(streams_of[1], (LAT1, D), 1.0, 6.0, ((0, 32),)),
        "tier_two_codes": normal_values(streams_of[2], (LAT2, D), 1.0, 6.0, ((0, 32),)),
        "tier_three_codes": normal_values(streams_of[3], (LAT3, D), 1.0, 6.0, ((0, 8),)),
        "tier_one_picks": draw_tier_one_picks(jax.random.fold_in(streams_of[15], 71), 0),
        "tier_two_picks": draw_tier_two_picks(jax.random.fold_in(streams_of[15], 71), 0),
        "tier_three_picks": draw_tier_three_picks(jax.random.fold_in(streams_of[15], 71), 0),
        "probe_matrix": normal_values(streams_of[7], (3, D, D), D ** -0.5, 0.25),
        "address_matrix": normal_values(streams_of[8], (3, D, D), D ** -0.5, 0.25),
        "content_matrix": normal_values(streams_of[9], (3, D, D), D ** -0.5, 0.25),
        "merge_matrix": normal_values(streams_of[10], (3, D, D), D ** -0.5, 0.25),
        "expand_matrix": normal_values(streams_of[11], (3, D, FFL), D ** -0.5, 0.25),
        "shrink_matrix": normal_values(streams_of[12], (3, FFL, D), FFL ** -0.5, 0.1875),
        "rescale_factors": jnp.clip(1.0 + 0.15 * jax.random.normal(streams_of[13], (3, 3, D), jnp.float32), 0.25, 1.75),
        "logit_scaling": jnp.clip(jnp.exp(jax.random.uniform(streams_of[14], (3, HEADS_ALL), jnp.float32, math.log(0.5), math.log(2.0))), 0.5, 2.0),
    }


eps = 1e-06

def normalize(values_in, gain_vec):
    return values_in * lax.rsqrt(lax.optimization_barrier(jnp.mean(values_in * values_in, axis=-1, keepdims=True)) + eps) * gain_vec

def per_head(values_in):
    dims_shape = values_in.shape
    grouped = values_in.reshape(dims_shape[:-1] + (HEADS_ALL, dims_shape[-1] // HEADS_ALL))
    grouped = grouped * lax.rsqrt(lax.optimization_barrier(jnp.mean(grouped * grouped, axis=-1, keepdims=True)) + eps)
    return grouped.reshape(dims_shape)

def refresh(latent, tier_ordinal, expand_matrix, shrink_matrix, rescale_factors):
    running_features = latent.astype(jnp.float32)
    mlp_in = normalize(running_features, rescale_factors[tier_ordinal, 1]).astype(jnp.bfloat16)
    hidden = jax.nn.silu(jnp.dot(mlp_in, expand_matrix[tier_ordinal], preferred_element_type=jnp.float32)).astype(jnp.bfloat16)
    renewed = (running_features + jnp.dot(hidden, shrink_matrix[tier_ordinal], preferred_element_type=jnp.float32)).astype(jnp.bfloat16)
    return lax.optimization_barrier(renewed)

def project(renewed, tier_ordinal, address_matrix, content_matrix, rescale_factors):
    kv_in = normalize(renewed.astype(jnp.float32), rescale_factors[tier_ordinal, 2]).astype(jnp.bfloat16)
    key_part = per_head(jnp.dot(kv_in, address_matrix[tier_ordinal], preferred_element_type=jnp.float32)).astype(jnp.bfloat16)
    value_part = jnp.dot(kv_in, content_matrix[tier_ordinal], preferred_element_type=jnp.float32).astype(jnp.bfloat16)
    return jnp.concatenate([key_part, value_part], axis=1)

def mix_across_tiers(running_features, gather_entries, tier_positions, tier_ordinal, probe_matrix, merge_matrix, rescale_factors, logit_scaling):
    row_count, feature = running_features.shape
    blocks = tier_positions.shape[0]
    group_dimension = feature // HEADS_ALL
    normed = normalize(running_features, rescale_factors[tier_ordinal, 0]).astype(jnp.bfloat16)
    queries = per_head(jnp.dot(normed, probe_matrix[tier_ordinal], preferred_element_type=jnp.float32)).astype(jnp.bfloat16)
    queries = queries.reshape(blocks, row_count // blocks, HEADS_ALL, group_dimension)
    chosen = jnp.take(gather_entries, tier_positions, axis=0)
    key_part = chosen[:, :, :feature].reshape(blocks, -1, HEADS_ALL, group_dimension)
    value_part = chosen[:, :, feature:].reshape(blocks, -1, HEADS_ALL, group_dimension)
    affinity_logits = jnp.einsum('bihd,bjhd->bhij', queries.astype(jnp.float32), key_part.astype(jnp.float32))
    affinity_logits = affinity_logits * (logit_scaling[tier_ordinal] / math.sqrt(group_dimension))[None, :, None, None]
    weights = jnp.exp(affinity_logits)
    weights = (weights / lax.optimization_barrier(jnp.sum(weights, axis=-1, keepdims=True))).astype(jnp.bfloat16)
    mixture = jnp.einsum('bhij,bjhd->bihd', weights.astype(jnp.float32), value_part.astype(jnp.float32))
    mixture = mixture.reshape(row_count, feature).astype(jnp.bfloat16)
    return running_features + jnp.dot(mixture, merge_matrix[tier_ordinal], preferred_element_type=jnp.float32)

def reference(pixel_features, tier_one_codes, tier_two_codes, tier_three_codes, tier_one_picks, tier_two_picks, tier_three_picks, probe_matrix, address_matrix, content_matrix, merge_matrix, expand_matrix, shrink_matrix, rescale_factors, logit_scaling):
    tables = []
    for tier_ordinal, latent in enumerate((tier_one_codes, tier_two_codes, tier_three_codes)):
        renewed = refresh(latent, tier_ordinal, expand_matrix, shrink_matrix, rescale_factors)
        tables.append(project(renewed, tier_ordinal, address_matrix, content_matrix, rescale_factors))
    group_count = NFINE // 4096
    states = pixel_features.astype(jnp.float32).reshape(group_count, 4096, D)
    first = tier_one_picks.reshape(group_count, 256, LIST)
    second = tier_two_picks.reshape(group_count, 256, LIST)
    third = tier_three_picks.reshape(group_count, 256, LIST)

    def one_group(packed):
        running_features, index_one, index_two, index_three = packed
        for tier_ordinal, (gather_entries, tier_positions) in enumerate(zip(tables, (index_one, index_two, index_three))):
            running_features = mix_across_tiers(running_features, gather_entries, tier_positions, tier_ordinal, probe_matrix, merge_matrix, rescale_factors, logit_scaling)
        return running_features.astype(jnp.bfloat16)
    result = lax.map(one_group, (states, first, second, third))
    return result.reshape(NFINE, D)
```

```python
import functools
import math

import jax
import jax.numpy as jnp
from jax import lax
from jax.experimental import pallas as pl
from jax.experimental.pallas import tpu as pltpu
from jax.sharding import PartitionSpec as P

eps = 1e-06
F32 = jnp.float32
BF16 = jnp.bfloat16
MESH = pl.DeviceIdType.MESH
NT = (((1,), (1,)), ((), ()))
SLOT = 8


def mm(a, b):
    return jnp.dot(a, b, preferred_element_type=F32)


def mm_nt(a, b):
    return lax.dot_general(a, b, NT, preferred_element_type=F32)


def iota(shape, dim):
    return lax.broadcasted_iota(jnp.int32, shape, dim)


def normalize(v, gain):
    return v * lax.rsqrt(jnp.mean(v * v, axis=-1, keepdims=True) + eps) * gain


def head_norm(v, mean_mat):
    half = mean_mat.shape[0]
    parts = []
    for at in range(0, v.shape[1], half):
        piece = v[:, at : at + half]
        mean = mm((piece * piece).astype(BF16), mean_mat)
        parts.append(piece * lax.rsqrt(mean + eps))
    return jnp.concatenate(parts, axis=1)


def expand_rows(counts, times):
    blocks, width = counts.shape
    return jnp.broadcast_to(counts[:, None, :], (blocks, times, width)).reshape(
        blocks * times, width
    )


def count_picks(picks, base, table, width):
    blocks, entries = picks.shape
    lane = iota((blocks, width), 1) % table
    total = jnp.zeros((blocks, width), F32)
    for j in range(entries):
        local = picks[:, j : j + 1] - base
        total = total + jnp.where(lane == local, 1.0, 0.0)
    return total


def kernel(
    sph_n, grp_n, heads, tile,
    x_hbm, c1_hbm, c2_ref, c3_ref, p1_ref, p2_ref, p3_ref,
    probe_hbm, address_hbm, content_hbm, merge_hbm, expand_hbm, shrink_hbm,
    gain_ref, scale_ref,
    out_hbm,
    x_v, q_v, out_v, tab1, slots2, slots3,
    probe, address, content, merge, expand, shrink,
    kq1, vq1, kb2, vb2, kb3, vb3, cnt1, cnt2, cnt3,
    w_sem, x_sem, out_sem, own_sem, s1_sem, r1_sem, s2_sem, r2_sem, s3_sem, r3_sem,
):
    rows, feature = x_v.shape
    block = c1_hbm.shape[0]
    group = rows // block
    hd = feature // heads
    quad = 4
    quads = heads // quad
    qf = quad * hd
    n2, n3 = c2_ref.shape[0], c3_ref.shape[0]
    t1, t2, t3 = tab1.shape[0], n2 * grp_n, n3 * sph_n
    sph, grp = lax.axis_index("sph"), lax.axis_index("grp")
    me = sph * grp_n + grp
    count = sph_n * grp_n
    right, left = (me + 1) % count, (me + count - 1) % count
    right_id = (right // grp_n, right % grp_n)
    left_id = (left // grp_n, left % grp_n)
    grp_ids = [(sph, (grp + k) % grp_n) for k in range(1, grp_n)]
    sph_ids = [((sph + k) % sph_n, grp) for k in range(1, sph_n)]

    barrier = pltpu.get_barrier_semaphore()
    for who in [right_id, left_id] + grp_ids + sph_ids:
        pl.semaphore_signal(barrier, inc=1, device_id=who, device_id_type=MESH)

    x_copy = pltpu.make_async_copy(x_hbm, x_v, x_sem)
    x_copy.start()
    own = pltpu.make_async_copy(c1_hbm, tab1.at[pl.ds(block, block)], own_sem)
    own.start()
    w_copies = {}
    pairs = {
        "probe": (probe_hbm, probe), "expand": (expand_hbm, expand),
        "shrink": (shrink_hbm, shrink), "address": (address_hbm, address),
        "content": (content_hbm, content), "merge": (merge_hbm, merge),
    }
    order = [("probe", 0)]
    for level in (1, 2):
        order += [(n, level) for n in ("expand", "shrink", "address", "content", "merge")]
    order += [(n, 0) for n in ("expand", "shrink", "address", "content", "merge")]
    order += [("probe", 1), ("probe", 2)]
    for i, (name, level) in enumerate(order):
        src, dst = pairs[name]
        cp = pltpu.make_async_copy(src.at[level], dst.at[level], w_sem.at[i])
        cp.start()
        w_copies[name, level] = cp

    slots2[grp] = jnp.concatenate(
        [c2_ref[...].astype(F32), jnp.zeros((SLOT - n2, feature), F32)], axis=0
    )
    slots3[sph] = jnp.concatenate(
        [c3_ref[...].astype(F32), jnp.zeros((SLOT - n3, feature), F32)], axis=0
    )

    pl.semaphore_wait(barrier, 2 + len(grp_ids) + len(sph_ids))
    remote = []
    for k, (who, lo) in enumerate(((right_id, 0), (left_id, 2 * block))):
        remote.append(pltpu.make_async_remote_copy(
            src_ref=c1_hbm, dst_ref=tab1.at[pl.ds(lo, block)],
            send_sem=s1_sem.at[k], recv_sem=r1_sem.at[k],
            device_id=who, device_id_type=MESH))
    for k, who in enumerate(grp_ids):
        remote.append(pltpu.make_async_remote_copy(
            src_ref=slots2.at[grp], dst_ref=slots2.at[grp],
            send_sem=s2_sem.at[k], recv_sem=r2_sem.at[k],
            device_id=who, device_id_type=MESH))
    for k, who in enumerate(sph_ids):
        remote.append(pltpu.make_async_remote_copy(
            src_ref=slots3.at[sph], dst_ref=slots3.at[sph],
            send_sem=s3_sem.at[k], recv_sem=r3_sem.at[k],
            device_id=who, device_id_type=MESH))
    for cp in remote:
        cp.start()

    mean_mat = jnp.where(
        iota((qf, qf), 0) // hd == iota((qf, qf), 1) // hd, 1.0 / hd, 0.0
    ).astype(BF16)

    cnt1[...] = count_picks(p1_ref[...], (me - 1) * block, t1, quad * t1)
    cnt2[...] = count_picks(p2_ref[...], sph * t2, t2, heads * t2)
    cnt3[...] = count_picks(p3_ref[...], 0, t3, heads * t3)

    x_copy.wait()
    w_copies["probe", 0].wait()

    def query(state, level):
        normed = normalize(state, gain_ref[level, 0:1, :]).astype(BF16)
        return head_norm(mm(normed, probe[level]), mean_mat).astype(BF16)

    def first_query(i, carry):
        at = pl.ds(pl.multiple_of(i * tile, tile), tile)
        q_v[at, :] = query(x_v[at, :].astype(F32), 0)
        return carry

    lax.fori_loop(0, rows // tile, first_query, 0)

    def scale_row(level):
        head = iota((1, feature), 1) // hd
        row = jnp.zeros((1, feature), F32)
        for h in range(heads):
            row = jnp.where(head == h, scale_ref[level, h], row)
        return row * (math.log2(math.e) / math.sqrt(hd))

    def latents(latent, level):
        for name in ("expand", "shrink", "address", "content"):
            w_copies[name, level].wait()
        mlp_in = normalize(latent, gain_ref[level, 1:2, :]).astype(BF16)
        hidden = mm(mlp_in, expand[level])
        hidden = (hidden / (1.0 + jnp.exp(-hidden))).astype(BF16)
        renewed = (latent + mm(hidden, shrink[level])).astype(BF16).astype(F32)
        kv_in = normalize(renewed, gain_ref[level, 2:3, :]).astype(BF16)
        key = head_norm(mm(kv_in, address[level]), mean_mat) * scale_row(level)
        return key, mm(kv_in, content[level])

    def compact(slots, n, table):
        count = slots.shape[0]
        flat = slots[...].reshape(count * SLOT, feature).astype(BF16)
        padded = max(table, 16)
        row, col = iota((padded, count * SLOT), 0), iota((padded, count * SLOT), 1)
        pick = jnp.where(col == row // n * SLOT + row % n, 1.0, 0.0).astype(BF16)
        return mm(pick, flat)

    def by_head(v, table, count):
        stacked = jnp.concatenate([v[:table]] * count, axis=0)
        mask = iota(stacked.shape, 0) // table == iota(stacked.shape, 1) // hd
        return jnp.where(mask, stacked, 0.0).astype(BF16)

    def small_level(slots, n, table, level, kb, vb):
        key, value = latents(compact(slots, n, table), level)
        kb[...] = by_head(key, table, heads)
        w_copies["merge", level].wait()
        vb[...] = mm(by_head(value, table, heads), merge[level]).astype(BF16)

    for cp in remote[2 : 2 + len(grp_ids)]:
        cp.wait_recv()
    small_level(slots2, n2, t2, 1, kb2, vb2)
    for cp in remote[2 + len(grp_ids) :]:
        cp.wait_recv()
    small_level(slots3, n3, t3, 2, kb3, vb3)
    own.wait()
    for cp in remote[:2]:
        cp.wait_recv()
    key, value = latents(tab1[...].astype(F32), 0)
    for a in range(quads):
        kq1[a] = by_head(key[:, a * qf : (a + 1) * qf], t1, quad)
        vq1[a, :, :qf] = by_head(value[:, a * qf : (a + 1) * qf], t1, quad)
        vq1[a, :, qf:] = by_head(jnp.ones((t1, qf), F32), t1, quad)
    w_copies["merge", 0].wait()
    w_copies["probe", 1].wait()
    w_copies["probe", 2].wait()

    def sum_mat(table):
        width = heads * table
        return jnp.where(
            iota((width, width), 0) // table == iota((width, width), 1) // table, 1.0, 0.0
        ).astype(BF16)

    sum2, sum3 = sum_mat(t2), sum_mat(t3)

    def small_mix(state, level, kb, vb, counts, sums):
        q = query(state, level)
        p = jnp.exp2(mm_nt(q, kb[...])) * counts
        total = mm(p.astype(BF16), sums)
        return state + mm((p / total).astype(BF16), vb[...])

    tb = tile // group

    def out_copy(i):
        at = pl.ds(pl.multiple_of(i * tile, tile), tile)
        return pltpu.make_async_copy(out_v.at[at], out_hbm.at[at], out_sem.at[i])

    def fine(i, carry):
        at = pl.ds(pl.multiple_of(i * tile, tile), tile)
        bt = pl.ds(pl.multiple_of(i * tb, tb), tb)
        state = x_v[at, :].astype(F32)
        counts = expand_rows(cnt1[bt, :], group)
        mixed = []
        for a in range(quads):
            p = jnp.exp2(mm_nt(q_v[at, a * qf : (a + 1) * qf], kq1[a])) * counts
            o = mm(p.astype(BF16), vq1[a])
            mixed.append((o[:, :qf] / o[:, qf:]).astype(BF16))
        state = state + mm(jnp.concatenate(mixed, axis=1), merge[0])
        state = small_mix(state, 1, kb2, vb2, expand_rows(cnt2[bt, :], group), sum2)
        state = small_mix(state, 2, kb3, vb3, expand_rows(cnt3[bt, :], group), sum3)
        out_v[at, :] = state.astype(BF16)
        out_copy(i).start()
        return carry

    lax.fori_loop(0, rows // tile, fine, 0)
    for i in range(rows // tile):
        out_copy(i).wait()
    for cp in remote:
        cp.wait_send()


def per_device(sph_n, grp_n, *args):
    (x, c1, c2, c3, p1, p2, p3, probe, address, content, merge, expand, shrink, gain, scale) = args
    rows, feature = x.shape
    levels, heads = scale.shape
    block = c1.shape[0]
    tile = 256
    t1, t2, t3 = 3 * block, c2.shape[0] * grp_n, c3.shape[0] * sph_n
    hd = feature // heads
    qf = 4 * hd
    quads = heads // 4
    any_ = pl.BlockSpec(memory_space=pl.ANY)
    vmem = pl.BlockSpec(memory_space=pltpu.VMEM)
    smem = pl.BlockSpec(memory_space=pltpu.SMEM)
    dma = pltpu.SemaphoreType.DMA
    return pl.pallas_call(
        functools.partial(kernel, sph_n, grp_n, heads, tile),
        out_shape=jax.ShapeDtypeStruct((rows, feature), BF16),
        in_specs=[any_, any_, vmem, vmem, vmem, vmem, vmem] + [any_] * 6 + [vmem, smem],
        out_specs=any_,
        scratch_shapes=[
            pltpu.VMEM((rows, feature), BF16),
            pltpu.VMEM((rows, feature), BF16),
            pltpu.VMEM((rows, feature), BF16),
            pltpu.VMEM((t1, feature), BF16),
            pltpu.VMEM((grp_n, SLOT, feature), F32),
            pltpu.VMEM((sph_n, SLOT, feature), F32),
            pltpu.VMEM(probe.shape, BF16),
            pltpu.VMEM(address.shape, BF16),
            pltpu.VMEM(content.shape, BF16),
            pltpu.VMEM(merge.shape, BF16),
            pltpu.VMEM(expand.shape, BF16),
            pltpu.VMEM(shrink.shape, BF16),
            pltpu.VMEM((quads, 4 * t1, qf), BF16),
            pltpu.VMEM((quads, 4 * t1, 2 * qf), BF16),
            pltpu.VMEM((heads * t2, feature), BF16),
            pltpu.VMEM((heads * t2, feature), BF16),
            pltpu.VMEM((heads * t3, feature), BF16),
            pltpu.VMEM((heads * t3, feature), BF16),
            pltpu.VMEM((block, 4 * t1), F32),
            pltpu.VMEM((block, heads * t2), F32),
            pltpu.VMEM((block, heads * t3), F32),
            dma((6 * levels,)), dma, dma((rows // tile,)), dma,
            dma((2,)), dma((2,)),
            dma((grp_n - 1,)), dma((grp_n - 1,)),
            dma((sph_n - 1,)), dma((sph_n - 1,)),
        ],
        compiler_params=pltpu.CompilerParams(
            collective_id=0, has_side_effects=True, vmem_limit_bytes=56 * 1024 * 1024
        ),
    )(x, c1, c2, c3, p1, p2, p3, probe, address, content, merge, expand, shrink, gain, scale)


def solution(mesh):
    both = P(("sph", "grp"), None)
    placed = (both, both, both, P("sph", None), both, both, both) + (P(),) * 8
    return jax.shard_map(
        functools.partial(per_device, mesh.shape["sph"], mesh.shape["grp"]),
        mesh=mesh, in_specs=placed, out_specs=both, check_vma=False,
    )
```

```python
import functools
import math

import jax
import jax.numpy as jnp
from jax import lax
from jax.experimental import pallas as pl
from jax.experimental.pallas import tpu as pltpu
from jax.sharding import PartitionSpec as P

eps = 1e-06
F32 = jnp.float32
BF16 = jnp.bfloat16
MESH = pl.DeviceIdType.MESH
NT = (((1,), (1,)), ((), ()))


def mm(a, b):
    return jnp.dot(a, b, preferred_element_type=F32)


def mm_nt(a, b):
    return lax.dot_general(a, b, NT, preferred_element_type=F32)


def iota(shape, dim):
    return lax.broadcasted_iota(jnp.int32, shape, dim)


def normalize(v, gain):
    return v * lax.rsqrt(jnp.mean(v * v, axis=-1, keepdims=True) + eps) * gain


def head_norm(v, mean_mat):
    half = mean_mat.shape[0]
    parts = []
    for at in range(0, v.shape[1], half):
        piece = v[:, at : at + half]
        mean = mm((piece * piece).astype(BF16), mean_mat)
        parts.append(piece * lax.rsqrt(mean + eps))
    return jnp.concatenate(parts, axis=1)


def expand_rows(counts, times):
    blocks, width = counts.shape
    return jnp.broadcast_to(counts[:, None, :], (blocks, times, width)).reshape(
        blocks * times, width
    )


def count_picks(picks_t, base, table, width):
    picks = jnp.transpose((picks_t - base).astype(F32)).astype(jnp.int32)
    blocks, entries = picks.shape
    lane = iota((blocks, width), 1) % table
    total = jnp.zeros((blocks, width), F32)
    for j in range(entries):
        local = picks[:, j : j + 1]
        total = total + jnp.where(lane == local, 1.0, 0.0)
    return total


def kernel(
    sph_n, grp_n, heads, tile,
    x_hbm, c1_hbm, c2_hbm, c3_hbm, p1_hbm, p2_hbm, p3_hbm,
    probe_hbm, address_hbm, content_hbm, merge_hbm, expand_hbm, shrink_hbm,
    gain_hbm, scale_hbm,
    out_ref,
    c2_ref, c3_ref, p1_ref, p2_ref, p3_ref, gain_ref, scale_ref,
    x_v, q_v, tab1, slots2, slots3,
    probe, address, content, merge, expand, shrink,
    kq1, vq1, kb2, vb2, kb3, vb3, cnt1, cnt2, cnt3,
    in_sem, w_sem, x_sem, own_sem, s1_sem, r1_sem, s2_sem, r2_sem, s3_sem, r3_sem,
):
    rows, feature = x_v.shape
    block = c1_hbm.shape[0]
    group = rows // block
    hd = feature // heads
    quad = 4
    quads = heads // quad
    qf = quad * hd
    n2, n3 = c2_hbm.shape[0], c3_hbm.shape[0]
    t1, t2, t3 = tab1.shape[0], n2 * grp_n, n3 * sph_n
    sph, grp = lax.axis_index("sph"), lax.axis_index("grp")
    me = sph * grp_n + grp
    count = sph_n * grp_n
    right, left = (me + 1) % count, (me + count - 1) % count
    right_id = (right // grp_n, right % grp_n)
    left_id = (left // grp_n, left % grp_n)
    grp_ids = [(sph, (grp + k) % grp_n) for k in range(1, grp_n)]
    sph_ids = [((sph + k) % sph_n, grp) for k in range(1, sph_n)]

    barrier = pltpu.get_barrier_semaphore()
    for who in [right_id, left_id] + grp_ids + sph_ids:
        pl.semaphore_signal(barrier, inc=1, device_id=who, device_id_type=MESH)

    small = []
    for i, (src, dst) in enumerate((
        (c3_hbm, c3_ref), (c2_hbm, c2_ref), (gain_hbm, gain_ref), (p1_hbm, p1_ref),
        (p2_hbm, p2_ref), (p3_hbm, p3_ref), (scale_hbm, scale_ref),
    )):
        cp = pltpu.make_async_copy(src, dst, in_sem.at[i])
        cp.start()
        small.append(cp)
    x_copy = pltpu.make_async_copy(x_hbm, x_v, x_sem)
    x_copy.start()
    own = pltpu.make_async_copy(c1_hbm, tab1.at[pl.ds(block, block)], own_sem)
    own.start()
    w_copies = {}
    pairs = {
        "probe": (probe_hbm, probe), "expand": (expand_hbm, expand),
        "shrink": (shrink_hbm, shrink), "address": (address_hbm, address),
        "content": (content_hbm, content), "merge": (merge_hbm, merge),
    }
    order = [("probe", 0)]
    for level in (1, 2):
        order += [(n, level) for n in ("expand", "shrink", "address", "content", "merge")]
    order += [(n, 0) for n in ("expand", "shrink", "address", "content", "merge")]
    order += [("probe", 1), ("probe", 2)]
    for i, (name, level) in enumerate(order):
        src, dst = pairs[name]
        w_copies[name, level] = pltpu.make_async_copy(
            src.at[level], dst.at[level], w_sem.at[i]
        )
    w_copies["probe", 0].start()

    small[0].wait()
    small[1].wait()
    slots2[grp] = c2_ref[...].astype(F32)
    slots3[sph] = c3_ref[...].astype(F32)

    pl.semaphore_wait(barrier, 2 + len(grp_ids) + len(sph_ids))
    remote = []
    for k, (who, lo) in enumerate(((right_id, 0), (left_id, 2 * block))):
        remote.append(pltpu.make_async_remote_copy(
            src_ref=c1_hbm, dst_ref=tab1.at[pl.ds(lo, block)],
            send_sem=s1_sem.at[k], recv_sem=r1_sem.at[k],
            device_id=who, device_id_type=MESH))
    for k, who in enumerate(grp_ids):
        remote.append(pltpu.make_async_remote_copy(
            src_ref=slots2.at[grp], dst_ref=slots2.at[grp],
            send_sem=s2_sem.at[k], recv_sem=r2_sem.at[k],
            device_id=who, device_id_type=MESH))
    for k, who in enumerate(sph_ids):
        remote.append(pltpu.make_async_remote_copy(
            src_ref=slots3.at[sph], dst_ref=slots3.at[sph],
            send_sem=s3_sem.at[k], recv_sem=r3_sem.at[k],
            device_id=who, device_id_type=MESH))
    for cp in remote:
        cp.start()
    for key in order[1:]:
        w_copies[key].start()
    for cp in small[2:]:
        cp.wait()

    mean_mat = jnp.where(
        iota((qf, qf), 0) // hd == iota((qf, qf), 1) // hd, 1.0 / hd, 0.0
    ).astype(BF16)

    cnt1[...] = count_picks(p1_ref[...], (me - 1) * block, t1, quad * t1)
    cnt2[...] = count_picks(p2_ref[...], sph * t2, t2, heads * t2)
    cnt3[...] = count_picks(p3_ref[...], 0, t3, heads * t3)

    x_copy.wait()
    w_copies["probe", 0].wait()

    def query(state, level):
        normed = normalize(state, gain_ref[level, 0:1, :]).astype(BF16)
        return head_norm(mm(normed, probe[level]), mean_mat).astype(BF16)

    def first_query(i, carry):
        at = pl.ds(pl.multiple_of(i * tile, tile), tile)
        q_v[at, :] = query(x_v[at, :].astype(F32), 0)
        return carry

    lax.fori_loop(0, rows // tile, first_query, 0)

    def scale_row(level):
        head = iota((1, feature), 1) // hd
        row = jnp.zeros((1, feature), F32)
        for h in range(heads):
            row = jnp.where(head == h, scale_ref[level : level + 1, h : h + 1], row)
        return row * (math.log2(math.e) / math.sqrt(hd))

    def latents(latent, level):
        for name in ("expand", "shrink", "address", "content"):
            w_copies[name, level].wait()
        mlp_in = normalize(latent, gain_ref[level, 1:2, :]).astype(BF16)
        hidden = mm(mlp_in, expand[level])
        hidden = (hidden / (1.0 + jnp.exp(-hidden))).astype(BF16)
        renewed = (latent + mm(hidden, shrink[level])).astype(BF16).astype(F32)
        kv_in = normalize(renewed, gain_ref[level, 2:3, :]).astype(BF16)
        key = head_norm(mm(kv_in, address[level]), mean_mat) * scale_row(level)
        return key, mm(kv_in, content[level])

    def compact(slots, table):
        pieces = [slots[k] for k in range(slots.shape[0])]
        if table < 16:
            pieces.append(jnp.zeros((16 - table, feature), F32))
        return jnp.concatenate(pieces, axis=0)

    def by_head(v, table, count):
        stacked = jnp.concatenate([v[:table]] * count, axis=0)
        mask = iota(stacked.shape, 0) // table == iota(stacked.shape, 1) // hd
        return jnp.where(mask, stacked, 0.0).astype(BF16)

    def small_level(slots, table, level, kb, vb):
        key, value = latents(compact(slots, table), level)
        kb[...] = by_head(key, table, heads)
        w_copies["merge", level].wait()
        vb[...] = mm(by_head(value, table, heads), merge[level]).astype(BF16)

    for cp in remote[2 : 2 + len(grp_ids)]:
        cp.wait_recv()
    small_level(slots2, t2, 1, kb2, vb2)
    for cp in remote[2 + len(grp_ids) :]:
        cp.wait_recv()
    small_level(slots3, t3, 2, kb3, vb3)
    own.wait()
    for cp in remote[:2]:
        cp.wait_recv()
    key, value = latents(tab1[...].astype(F32), 0)
    for a in range(quads):
        kq1[a] = by_head(key[:, a * qf : (a + 1) * qf], t1, quad)
        vq1[a, :, :qf] = by_head(value[:, a * qf : (a + 1) * qf], t1, quad)
        vq1[a, :, qf:] = by_head(jnp.ones((t1, qf), F32), t1, quad)
    w_copies["merge", 0].wait()
    w_copies["probe", 1].wait()
    w_copies["probe", 2].wait()

    def sum_mat(table):
        width = heads * table
        return jnp.where(
            iota((width, width), 0) // table == iota((width, width), 1) // table, 1.0, 0.0
        ).astype(BF16)

    sum2, sum3 = sum_mat(t2), sum_mat(t3)

    def small_mix(state, level, kb, vb, counts, sums):
        q = query(state, level)
        p = jnp.exp2(mm_nt(q, kb[...])) * counts
        total = mm(p.astype(BF16), sums)
        return state + mm((p / total).astype(BF16), vb[...])

    tb = tile // group

    def fine(i, carry):
        at = pl.ds(pl.multiple_of(i * tile, tile), tile)
        bt = pl.ds(pl.multiple_of(i * tb, tb), tb)
        state = x_v[at, :].astype(F32)
        counts = expand_rows(cnt1[bt, :], group)
        mixed = []
        for a in range(quads):
            p = jnp.exp2(mm_nt(q_v[at, a * qf : (a + 1) * qf], kq1[a])) * counts
            o = mm(p.astype(BF16), vq1[a])
            mixed.append((o[:, :qf] / o[:, qf:]).astype(BF16))
        state = state + mm(jnp.concatenate(mixed, axis=1), merge[0])
        state = small_mix(state, 1, kb2, vb2, expand_rows(cnt2[bt, :], group), sum2)
        state = small_mix(state, 2, kb3, vb3, expand_rows(cnt3[bt, :], group), sum3)
        out_ref[at, :] = state.astype(BF16)
        return carry

    lax.fori_loop(0, rows // tile, fine, 0)
    for cp in remote:
        cp.wait_send()


def per_device(sph_n, grp_n, *args):
    (x, c1, c2, c3, p1, p2, p3, probe, address, content, merge, expand, shrink, gain, scale) = args
    rows, feature = x.shape
    levels, heads = scale.shape
    block = c1.shape[0]
    tile = 256
    t1, t2, t3 = 3 * block, c2.shape[0] * grp_n, c3.shape[0] * sph_n
    hd = feature // heads
    qf = 4 * hd
    quads = heads // 4
    any_ = pl.BlockSpec(memory_space=pl.ANY)
    dma = pltpu.SemaphoreType.DMA
    return pl.pallas_call(
        functools.partial(kernel, sph_n, grp_n, heads, tile),
        out_shape=pltpu.VMEM((rows, feature), BF16),
        in_specs=[any_] * 15,
        out_specs=pl.BlockSpec(memory_space=pltpu.VMEM),
        scratch_shapes=[
            pltpu.VMEM(c2.shape, BF16),
            pltpu.VMEM(c3.shape, BF16),
            pltpu.VMEM(p1.shape[::-1], jnp.int32),
            pltpu.VMEM(p2.shape[::-1], jnp.int32),
            pltpu.VMEM(p3.shape[::-1], jnp.int32),
            pltpu.VMEM(gain.shape, F32),
            pltpu.VMEM(scale.shape, F32),
            pltpu.VMEM((rows, feature), BF16),
            pltpu.VMEM((rows, feature), BF16),
            pltpu.VMEM((t1, feature), BF16),
            pltpu.VMEM((grp_n,) + c2.shape, F32),
            pltpu.VMEM((sph_n,) + c3.shape, F32),
            pltpu.VMEM(probe.shape, BF16),
            pltpu.VMEM(address.shape, BF16),
            pltpu.VMEM(content.shape, BF16),
            pltpu.VMEM(merge.shape, BF16),
            pltpu.VMEM(expand.shape, BF16),
            pltpu.VMEM(shrink.shape, BF16),
            pltpu.VMEM((quads, 4 * t1, qf), BF16),
            pltpu.VMEM((quads, 4 * t1, 2 * qf), BF16),
            pltpu.VMEM((heads * t2, feature), BF16),
            pltpu.VMEM((heads * t2, feature), BF16),
            pltpu.VMEM((heads * t3, feature), BF16),
            pltpu.VMEM((heads * t3, feature), BF16),
            pltpu.VMEM((block, 4 * t1), F32),
            pltpu.VMEM((block, heads * t2), F32),
            pltpu.VMEM((block, heads * t3), F32),
            dma((7,)), dma((6 * levels,)), dma, dma,
            dma((2,)), dma((2,)),
            dma((grp_n - 1,)), dma((grp_n - 1,)),
            dma((sph_n - 1,)), dma((sph_n - 1,)),
        ],
        compiler_params=pltpu.CompilerParams(
            collective_id=0, has_side_effects=True, vmem_limit_bytes=122 * 512 * 1024
        ),
    )(x, c1, c2, c3, p1.T, p2.T, p3.T, probe, address, content, merge, expand, shrink, gain, scale)


def solution(mesh):
    both = P(("sph", "grp"), None)
    placed = (both, both, both, P("sph", None), both, both, both) + (P(),) * 8
    return jax.shard_map(
        functools.partial(per_device, mesh.shape["sph"], mesh.shape["grp"]),
        mesh=mesh, in_specs=placed, out_specs=both, check_vma=False,
    )
```

```python
import functools
import math

import jax
import jax.numpy as jnp
from jax import lax
from jax.experimental import pallas as pl
from jax.experimental.pallas import tpu as pltpu
from jax.sharding import PartitionSpec as P

eps = 1e-06
F32 = jnp.float32
BF16 = jnp.bfloat16
MESH = pl.DeviceIdType.MESH
NT = (((1,), (1,)), ((), ()))


def mm(a, b):
    return jnp.dot(a, b, preferred_element_type=F32)


def mm_nt(a, b):
    return lax.dot_general(a, b, NT, preferred_element_type=F32)


def iota(shape, dim):
    return lax.broadcasted_iota(jnp.int32, shape, dim)


def normalize(v, gain):
    return v * lax.rsqrt(jnp.mean(v * v, axis=-1, keepdims=True) + eps) * gain


def head_norm(v, mean_mat):
    half = mean_mat.shape[0]
    parts = []
    for at in range(0, v.shape[1], half):
        piece = v[:, at : at + half]
        mean = mm((piece * piece).astype(BF16), mean_mat)
        parts.append(piece * lax.rsqrt(mean + eps))
    return jnp.concatenate(parts, axis=1)


def expand_rows(counts, times):
    blocks, width = counts.shape
    return jnp.broadcast_to(counts[:, None, :], (blocks, times, width)).reshape(
        blocks * times, width
    )


def count_picks(picks_t, base, table, width):
    picks = jnp.transpose((picks_t - base).astype(F32)).astype(jnp.int32)
    blocks, entries = picks.shape
    lane = iota((blocks, width), 1) % table
    total = jnp.zeros((blocks, width), F32)
    for j in range(entries):
        local = picks[:, j : j + 1]
        total = total + jnp.where(lane == local, 1.0, 0.0)
    return total


def kernel(
    sph_n, grp_n, heads, tile,
    x_hbm, c1_hbm, c2_hbm, c3_hbm, p1_hbm, p2_hbm, p3_hbm,
    probe_hbm, address_hbm, content_hbm, merge_hbm, expand_hbm, shrink_hbm,
    gain_hbm, scale_hbm,
    out_ref,
    c2_ref, c3_ref, p1_ref, p2_ref, p3_ref, gain_ref, scale_ref,
    x_v, q_v, tab1, slots2, slots3,
    probe, address, content, merge, expand, shrink,
    kq1, vq1, kb2, vb2, kb3, vb3, cnt1, cnt2, cnt3,
    in_sem, w_sem, x_sem, own_sem, s1_sem, r1_sem, s2_sem, r2_sem, s3_sem, r3_sem,
):
    rows, feature = x_v.shape
    block = c1_hbm.shape[0]
    group = rows // block
    hd = feature // heads
    quad = 4
    quads = heads // quad
    qf = quad * hd
    n2, n3 = c2_hbm.shape[0], c3_hbm.shape[0]
    t1, t2, t3 = tab1.shape[0], n2 * grp_n, n3 * sph_n
    sph, grp = lax.axis_index("sph"), lax.axis_index("grp")
    me = sph * grp_n + grp
    count = sph_n * grp_n
    right, left = (me + 1) % count, (me + count - 1) % count
    right_id = (right // grp_n, right % grp_n)
    left_id = (left // grp_n, left % grp_n)
    grp_ids = [(sph, (grp + k) % grp_n) for k in range(1, grp_n)]
    sph_ids = [((sph + k) % sph_n, grp) for k in range(1, sph_n)]

    barrier = pltpu.get_barrier_semaphore()
    for who in [right_id, left_id] + grp_ids + sph_ids:
        pl.semaphore_signal(barrier, inc=1, device_id=who, device_id_type=MESH)

    small = []
    for i, (src, dst) in enumerate((
        (c3_hbm, c3_ref), (c2_hbm, c2_ref), (gain_hbm, gain_ref), (p1_hbm, p1_ref),
        (p2_hbm, p2_ref), (p3_hbm, p3_ref), (scale_hbm, scale_ref),
    )):
        cp = pltpu.make_async_copy(src, dst, in_sem.at[i])
        cp.start()
        small.append(cp)
    x_copy = pltpu.make_async_copy(x_hbm, x_v, x_sem)
    x_copy.start()
    own = pltpu.make_async_copy(c1_hbm, tab1.at[pl.ds(block, block)], own_sem)
    own.start()
    w_copies = {}
    pairs = {
        "probe": (probe_hbm, probe), "expand": (expand_hbm, expand),
        "shrink": (shrink_hbm, shrink), "address": (address_hbm, address),
        "content": (content_hbm, content), "merge": (merge_hbm, merge),
    }
    order = [("probe", 0)]
    for level in (1, 2):
        order += [(n, level) for n in ("expand", "shrink", "address", "content", "merge")]
    order += [(n, 0) for n in ("expand", "shrink", "address", "content", "merge")]
    order += [("probe", 1), ("probe", 2)]
    for i, (name, level) in enumerate(order):
        src, dst = pairs[name]
        w_copies[name, level] = pltpu.make_async_copy(
            src.at[level], dst.at[level], w_sem.at[i]
        )
    w_copies["probe", 0].start()

    small[0].wait()
    small[1].wait()
    slots2[grp] = c2_ref[...].astype(F32)
    slots3[sph] = c3_ref[...].astype(F32)

    pl.semaphore_wait(barrier, 2 + len(grp_ids) + len(sph_ids))
    remote = []
    for k, (who, lo) in enumerate(((right_id, 0), (left_id, 2 * block))):
        remote.append(pltpu.make_async_remote_copy(
            src_ref=c1_hbm, dst_ref=tab1.at[pl.ds(lo, block)],
            send_sem=s1_sem.at[k], recv_sem=r1_sem.at[k],
            device_id=who, device_id_type=MESH))
    for k, who in enumerate(grp_ids):
        remote.append(pltpu.make_async_remote_copy(
            src_ref=slots2.at[grp], dst_ref=slots2.at[grp],
            send_sem=s2_sem.at[k], recv_sem=r2_sem.at[k],
            device_id=who, device_id_type=MESH))
    for k, who in enumerate(sph_ids):
        remote.append(pltpu.make_async_remote_copy(
            src_ref=slots3.at[sph], dst_ref=slots3.at[sph],
            send_sem=s3_sem.at[k], recv_sem=r3_sem.at[k],
            device_id=who, device_id_type=MESH))
    for cp in remote:
        cp.start()
    for key in order[1:]:
        w_copies[key].start()
    for cp in small[2:]:
        cp.wait()

    mean_mat = jnp.where(
        iota((qf, qf), 0) // hd == iota((qf, qf), 1) // hd, 1.0 / hd, 0.0
    ).astype(BF16)

    cnt1[...] = count_picks(p1_ref[...], (me - 1) * block, t1, quad * t1)
    cnt2[...] = count_picks(p2_ref[...], sph * t2, t2, heads * t2)
    cnt3[...] = count_picks(p3_ref[...], 0, t3, heads * t3)

    x_copy.wait()
    w_copies["probe", 0].wait()

    def query(state, level):
        normed = normalize(state, gain_ref[level, 0:1, :]).astype(BF16)
        return head_norm(mm(normed, probe[level]), mean_mat).astype(BF16)

    def first_query(i, carry):
        at = pl.ds(pl.multiple_of(i * tile, tile), tile)
        q_v[at, :] = query(x_v[at, :].astype(F32), 0)
        return carry

    lax.fori_loop(0, rows // tile, first_query, 0)

    def scale_row(level):
        head = iota((1, feature), 1) // hd
        row = jnp.zeros((1, feature), F32)
        for h in range(heads):
            row = jnp.where(head == h, scale_ref[level : level + 1, h : h + 1], row)
        return row * (math.log2(math.e) / math.sqrt(hd))

    def latents(latent, level):
        for name in ("expand", "shrink", "address", "content"):
            w_copies[name, level].wait()
        mlp_in = normalize(latent, gain_ref[level, 1:2, :]).astype(BF16)
        hidden = mm(mlp_in, expand[level])
        hidden = (hidden / (1.0 + jnp.exp(-hidden))).astype(BF16)
        renewed = (latent + mm(hidden, shrink[level])).astype(BF16).astype(F32)
        kv_in = normalize(renewed, gain_ref[level, 2:3, :]).astype(BF16)
        key = head_norm(mm(kv_in, address[level]), mean_mat) * scale_row(level)
        return key, mm(kv_in, content[level])

    def compact(slots, table):
        pieces = [slots[k] for k in range(slots.shape[0])]
        if table < 16:
            pieces.append(jnp.zeros((16 - table, feature), F32))
        return jnp.concatenate(pieces, axis=0)

    def by_head(v, table, count):
        stacked = jnp.concatenate([v[:table]] * count, axis=0)
        mask = iota(stacked.shape, 0) // table == iota(stacked.shape, 1) // hd
        return jnp.where(mask, stacked, 0.0).astype(BF16)

    def small_level(slots, table, level, kb, vb):
        key, value = latents(compact(slots, table), level)
        kb[...] = by_head(key, table, heads).T
        w_copies["merge", level].wait()
        vb[...] = mm(by_head(value, table, heads), merge[level]).astype(BF16)

    for cp in remote[2 : 2 + len(grp_ids)]:
        cp.wait_recv()
    small_level(slots2, t2, 1, kb2, vb2)
    for cp in remote[2 + len(grp_ids) :]:
        cp.wait_recv()
    small_level(slots3, t3, 2, kb3, vb3)
    own.wait()
    for cp in remote[:2]:
        cp.wait_recv()
    key, value = latents(tab1[...].astype(F32), 0)
    for a in range(quads):
        kq1[a] = by_head(key[:, a * qf : (a + 1) * qf], t1, quad).T
        vq1[a, :, :qf] = by_head(value[:, a * qf : (a + 1) * qf], t1, quad)
        vq1[a, :, qf:] = by_head(jnp.ones((t1, qf), F32), t1, quad)
    w_copies["merge", 0].wait()
    w_copies["probe", 1].wait()
    w_copies["probe", 2].wait()

    def sum_mat(table):
        width = heads * table
        return jnp.where(
            iota((width, width), 0) // table == iota((width, width), 1) // table, 1.0, 0.0
        ).astype(BF16)

    sum2, sum3 = sum_mat(t2), sum_mat(t3)

    def small_mix(state, level, kb, vb, counts, sums):
        q = query(state, level)
        p = jnp.exp2(mm(q, kb[...])) * counts
        total = mm(p.astype(BF16), sums)
        return state + mm((p * pl.reciprocal(total, approx=True)).astype(BF16), vb[...])

    tb = tile // group

    def fine(i, carry):
        at = pl.ds(pl.multiple_of(i * tile, tile), tile)
        bt = pl.ds(pl.multiple_of(i * tb, tb), tb)
        state = x_v[at, :].astype(F32)
        counts = expand_rows(cnt1[bt, :], group)
        mixed = []
        for a in range(quads):
            p = jnp.exp2(mm(q_v[at, a * qf : (a + 1) * qf], kq1[a])) * counts
            o = mm(p.astype(BF16), vq1[a])
            mixed.append((o[:, :qf] * pl.reciprocal(o[:, qf:], approx=True)).astype(BF16))
        state = state + mm(jnp.concatenate(mixed, axis=1), merge[0])
        state = small_mix(state, 1, kb2, vb2, expand_rows(cnt2[bt, :], group), sum2)
        state = small_mix(state, 2, kb3, vb3, expand_rows(cnt3[bt, :], group), sum3)
        out_ref[at, :] = state.astype(BF16)
        return carry

    lax.fori_loop(0, rows // tile, fine, 0)
    for cp in remote:
        cp.wait_send()


def per_device(sph_n, grp_n, *args):
    (x, c1, c2, c3, p1, p2, p3, probe, address, content, merge, expand, shrink, gain, scale) = args
    rows, feature = x.shape
    levels, heads = scale.shape
    block = c1.shape[0]
    tile = rows
    t1, t2, t3 = 3 * block, c2.shape[0] * grp_n, c3.shape[0] * sph_n
    hd = feature // heads
    qf = 4 * hd
    quads = heads // 4
    any_ = pl.BlockSpec(memory_space=pl.ANY)
    dma = pltpu.SemaphoreType.DMA
    return pl.pallas_call(
        functools.partial(kernel, sph_n, grp_n, heads, tile),
        out_shape=pltpu.VMEM((rows, feature), BF16),
        in_specs=[any_] * 15,
        out_specs=pl.BlockSpec(memory_space=pltpu.VMEM),
        scratch_shapes=[
            pltpu.VMEM(c2.shape, BF16),
            pltpu.VMEM(c3.shape, BF16),
            pltpu.VMEM(p1.shape[::-1], jnp.int32),
            pltpu.VMEM(p2.shape[::-1], jnp.int32),
            pltpu.VMEM(p3.shape[::-1], jnp.int32),
            pltpu.VMEM(gain.shape, F32),
            pltpu.VMEM(scale.shape, F32),
            pltpu.VMEM((rows, feature), BF16),
            pltpu.VMEM((rows, feature), BF16),
            pltpu.VMEM((t1, feature), BF16),
            pltpu.VMEM((grp_n,) + c2.shape, F32),
            pltpu.VMEM((sph_n,) + c3.shape, F32),
            pltpu.VMEM(probe.shape, BF16),
            pltpu.VMEM(address.shape, BF16),
            pltpu.VMEM(content.shape, BF16),
            pltpu.VMEM(merge.shape, BF16),
            pltpu.VMEM(expand.shape, BF16),
            pltpu.VMEM(shrink.shape, BF16),
            pltpu.VMEM((quads, qf, 4 * t1), BF16),
            pltpu.VMEM((quads, 4 * t1, 2 * qf), BF16),
            pltpu.VMEM((feature, heads * t2), BF16),
            pltpu.VMEM((heads * t2, feature), BF16),
            pltpu.VMEM((feature, heads * t3), BF16),
            pltpu.VMEM((heads * t3, feature), BF16),
            pltpu.VMEM((block, 4 * t1), F32),
            pltpu.VMEM((block, heads * t2), F32),
            pltpu.VMEM((block, heads * t3), F32),
            dma((7,)), dma((6 * levels,)), dma, dma,
            dma((2,)), dma((2,)),
            dma((grp_n - 1,)), dma((grp_n - 1,)),
            dma((sph_n - 1,)), dma((sph_n - 1,)),
        ],
        compiler_params=pltpu.CompilerParams(
            collective_id=0, has_side_effects=True, vmem_limit_bytes=122 * 512 * 1024
        ),
    )(x, c1, c2, c3, p1.T, p2.T, p3.T, probe, address, content, merge, expand, shrink, gain, scale)


def solution(mesh):
    both = P(("sph", "grp"), None)
    placed = (both, both, both, P("sph", None), both, both, both) + (P(),) * 8
    return jax.shard_map(
        functools.partial(per_device, mesh.shape["sph"], mesh.shape["grp"]),
        mesh=mesh, in_specs=placed, out_specs=both, check_vma=False,
    )
```
